32 devices in a mesh: seq: 8 (over z, y), mp: 4 (over x, core).
Axes of the slice: x: 2, y: 2, z: 4, core: 2. Of those that a mesh axis runs over, the one named last changes fastest.
Arguments:
- hidden: bfloat16 [8192, 4096], P('seq', 'mp')
- picked: int32 [1024], P('seq'), may hold values from 0 to 8191, as said below
- target: int32 [8192], P('seq'), may hold values from -1 to 1023, as said below
- norm_gain: bfloat16 [4096], replicated, may hold values from 0.099609375 to 1.8984375
- router_weight: bfloat16 [4096], replicated, may hold values from -0.1875 to 0.1875
- w_query: bfloat16 [4096, 2048], P('seq', 'mp')
- w_key: bfloat16 [4096, 2048], P('seq', 'mp')
- w_value: bfloat16 [4096, 2048], P('seq', 'mp'), may hold values from -0.1875 to 0.1875
- w_out: bfloat16 [2048, 4096], P(None, 'mp'), may hold values from -0.125 to 0.125
Outputs:
- mixed: bfloat16 [8192, 4096], P('seq', 'mp')
The draws below stay inside these ranges and needn't reach their ends.
Inputs may be any that keep to these rules, and one draw needn't show every extreme that they name: `picked`: entry g holds the position of the routed token of rank (g mod 128) * 8 + g div 128, ranks counting the 1024 routed positions in increasing order. target[p] = g where picked[g] = p, and -1 where p is not routed; each aligned block of 1024 positions holds at most 256 routed ones, and some block holds exactly 256.
All inputs are finite; a program needn't handle non-finite values.
Results may differ from the reference program's by a relative error of at most 0.004.
Values may be sent and summed in bfloat16 or wider, within the bound.
A program may use at most 128 MiB of HBM per device.

```python
import math
import jax
import jax.numpy as jnp
from jax import lax

D = 4096
HEADS = 16
HEAD_DIM = 128
TOK_DEV = 1024
SOURCES = 8
SEL_DEV = 128
SEQ = 8192
SEL = 1024


def selection(key):
    first, second, third = jax.random.split(key, 3)
    half = SOURCES // 2
    order = jax.random.permutation(first, SOURCES)
    shifts = jax.random.randint(second, (half,), 0, SEL_DEV + 1)
    shifts = shifts.at[0].set(SEL_DEV)
    counts = jnp.full((SOURCES,), SEL_DEV, jnp.int32)
    counts = counts.at[order[:half]].add(shifts).at[order[half:2 * half]].add(-shifts)
    noise = jax.random.randint(third, (SOURCES, TOK_DEV), 0, 2 ** 20)
    scores = noise * TOK_DEV + jnp.arange(TOK_DEV, dtype=jnp.int32)[None, :]
    ordering = jnp.argsort(scores, axis=1)
    ranking = jnp.argsort(ordering, axis=1)
    chosen = (ranking < counts[:, None]).reshape(SEQ)
    rank = jnp.cumsum(chosen.astype(jnp.int32)) - 1
    compact = rank % SOURCES * SEL_DEV + rank // SOURCES
    target = jnp.where(chosen, compact, -1).astype(jnp.int32)
    spots = jnp.where(chosen, compact, SEL)
    picked = jnp.zeros((SEL,), jnp.int32).at[spots].set(jnp.arange(SEQ, dtype=jnp.int32), mode='drop')
    return (picked, target)


def shared_projection(key):
    return jax.random.normal(key, (D, HEADS * HEAD_DIM), jnp.float32)


def mixed_projection(common, key, shared_part, own_part):
    own = jax.random.normal(key, (D, HEADS * HEAD_DIM), jnp.float32)
    return ((shared_part * common + own_part * own) / math.sqrt(D)).astype(jnp.bfloat16)


def draw_picked(key, part):
    shared = selection(key)
    return shared[0]


def draw_target(key, part):
    shared = selection(key)
    return shared[1]


def draw_w_query(key, part):
    common = shared_projection(key)
    key = jax.random.fold_in(key, 2)
    return mixed_projection(common, key, 0.6, 0.8)


def draw_w_key(key, part):
    common = shared_projection(key)
    key = jax.random.fold_in(key, 3)
    return mixed_projection(common, key, 0.6, 0.8)


def draw_hidden(key, part):
    key = jax.random.fold_in(key, 5)
    first = jax.random.fold_in(key, 0)
    base = jax.random.normal(first, (SEQ, D), jnp.float32)
    return base.astype(jnp.bfloat16)


def level_of(stream_key, shape, pieces, low, high):
    def one(axis_at, parts):
        steps = jax.random.uniform(jax.random.fold_in(jax.random.fold_in(stream_key, 6), axis_at), (parts,), jnp.float32, low / len(pieces), high / len(pieces))
        return jnp.repeat(jnp.exp(steps), shape[axis_at] // parts).reshape((-1,) + (1,) * (len(shape) - axis_at - 1))

    factor_of = one(*pieces[0])
    for cut in pieces[1:]:
        factor_of = factor_of * one(*cut)
    return factor_of


def normal_values(key, shape, deviation, limit, cuts=(), kind=jnp.bfloat16):
    entries = deviation * jax.random.normal(key, shape, jnp.float32)
    if cuts:
        entries = entries * level_of(key, shape, cuts, -0.22, 0.18)
    return jnp.clip(entries, -limit, limit).astype(kind)


def setup_inputs(seed: int = 0) -> dict:
    key_list = jax.random.split(jax.random.key(seed), 10)
    return {
        "hidden": draw_hidden(jax.random.fold_in(key_list[9], 71), 0),
        "picked": draw_picked(jax.random.fold_in(key_list[9], 71), 0),
        "target": draw_target(jax.random.fold_in(key_list[9], 71), 0),
        "norm_gain": jnp.clip(1.0 + 0.18 * jax.random.normal(key_list[3], (D,), jnp.float32), 0.099609375, 1.8984375).astype(jnp.bfloat16),
        "router_weight": normal_values(key_list[4], (D,), (D // 4) ** -0.5, 0.1875),
        "w_query": draw_w_query(jax.random.fold_in(key_list[9], 71), 0),
        "w_key": draw_w_key(jax.random.fold_in(key_list[9], 71), 0),
        "w_value": normal_values(key_list[7], (D, HEADS * HEAD_DIM), (D // 4) ** -0.5, 0.1875, ((0, 8), (1, 4))),
        "w_out": normal_values(key_list[8], (HEADS * HEAD_DIM, D), (HEADS * HEAD_DIM) ** -0.5, 0.125, ((1, 4),)),
    }


def rotate(vec, positions):
    half = vec.shape[-1] // 2
    freq = jnp.exp(-math.log(10000.0) * (2.0 * jnp.arange(half, dtype=jnp.float32) / vec.shape[-1]))
    angle = positions.astype(jnp.float32)[:, None] * freq[None, :]
    cosine = jnp.cos(angle)[:, None, :]
    sine = jnp.sin(angle)[:, None, :]
    first = vec[..., :half]
    second = vec[..., half:]
    return jnp.concatenate([first * cosine - second * sine, second * cosine + first * sine], axis=-1)

def reference(hidden, picked, target, norm_gain, router_weight, w_query, w_key, w_value, w_out):
    rows = hidden[picked]
    whole = rows.astype(jnp.float32)
    inverse = lax.rsqrt(lax.optimization_barrier(jnp.mean(whole * whole, axis=-1, keepdims=True)) + 1e-05)
    normed = (whole * inverse * norm_gain.astype(jnp.float32)).astype(jnp.bfloat16)
    gate = jax.nn.sigmoid(jnp.dot(rows, router_weight, preferred_element_type=jnp.float32))
    query = jnp.dot(normed, w_query, preferred_element_type=jnp.float32).reshape(SEL, HEADS, HEAD_DIM)
    keys = jnp.dot(normed, w_key, preferred_element_type=jnp.float32).reshape(SEL, HEADS, HEAD_DIM)
    values = jnp.dot(normed, w_value, preferred_element_type=jnp.float32).reshape(SEL, HEADS, HEAD_DIM)
    query = rotate(query, picked).astype(jnp.bfloat16)
    keys = rotate(keys, picked).astype(jnp.bfloat16)
    values = values.astype(jnp.bfloat16)
    index = jnp.arange(SEL, dtype=jnp.int32)
    rank = index % SEL_DEV * SOURCES + index // SEL_DEV
    allowed = rank[None, :] <= rank[:, None]
    scale = 1.0 / math.sqrt(HEAD_DIM)

    def one_head(operands):
        head_q, head_k, head_v = operands
        scores = jnp.dot(head_q, head_k.T, preferred_element_type=jnp.float32) * scale
        scores = jnp.where(allowed, scores, -1e+30)
        top = lax.optimization_barrier(jnp.max(scores, axis=-1, keepdims=True))
        weights = jnp.where(allowed, jnp.exp(scores - top), 0.0)
        total = lax.optimization_barrier(jnp.sum(weights, axis=-1, keepdims=True))
        summed = jnp.dot(weights.astype(jnp.bfloat16), head_v, preferred_element_type=jnp.float32)
        return summed / total
    stacked = (jnp.moveaxis(query, 1, 0), jnp.moveaxis(keys, 1, 0), jnp.moveaxis(values, 1, 0))
    heads_out = lax.map(one_head, stacked)
    attended = jnp.moveaxis(heads_out, 0, 1).reshape(SEL, HEADS * HEAD_DIM).astype(jnp.bfloat16)
    update = jnp.dot(attended, w_out, preferred_element_type=jnp.float32)
    new_rows = (whole + gate[:, None] * update).astype(jnp.bfloat16)
    live = target >= 0
    taken = new_rows[jnp.where(live, target, 0).astype(jnp.int32)]
    return jnp.where(live[:, None], taken, hidden)
```

```python
import math

import jax
import jax.numpy as jnp
from jax import lax
from jax.experimental import pallas as pl
from jax.experimental.pallas import tpu as pltpu
from jax.sharding import PartitionSpec as P

HEAD_DIM = 128
MESH = pl.DeviceIdType.MESH
BF = jnp.bfloat16
F32 = jnp.float32


def rotate(vec, positions):
    half = vec.shape[-1] // 2
    freq = jnp.exp(-math.log(10000.0) * (2.0 * jnp.arange(half, dtype=jnp.float32) / vec.shape[-1]))
    angle = positions.astype(jnp.float32)[:, None] * freq[None, :]
    cosine = jnp.cos(angle)[:, None, :]
    sine = jnp.sin(angle)[:, None, :]
    first = vec[..., :half]
    second = vec[..., half:]
    return jnp.concatenate(
        [first * cosine - second * sine, second * cosine + first * sine], axis=-1
    )


def general(hidden, picked, target, norm_gain, router_weight, w_query, w_key, w_value, w_out):
    shards = lax.axis_size("seq")
    here = lax.axis_index("seq")
    tok_rows = hidden.shape[0]
    part_width = hidden.shape[1]
    sel_rows = picked.shape[0]
    bucket = (2 * sel_rows + shards - 1) // shards
    live = target >= 0
    dest = jnp.where(live, target // sel_rows, shards)
    cell = dest * bucket + jnp.where(live, target % sel_rows, 0) % bucket
    table = jnp.full((shards * bucket,), tok_rows, jnp.int32)
    table = table.at[cell].set(jnp.arange(tok_rows, dtype=jnp.int32), mode="drop")
    padded = jnp.concatenate([hidden, jnp.zeros((1, part_width), hidden.dtype)], axis=0)
    outgoing = padded[table].reshape(shards, bucket, part_width)
    slots = jnp.arange(sel_rows, dtype=jnp.int32)
    source = picked // tok_rows
    fetch = source * bucket + slots % bucket
    arrived = lax.all_to_all(outgoing, "seq", split_axis=0, concat_axis=0, tiled=True)
    own_rows = arrived.reshape(shards * bucket, part_width)[fetch]
    full_rows = lax.all_gather(own_rows, "mp", axis=1, tiled=True)
    whole = full_rows.astype(jnp.float32)
    inverse = lax.rsqrt(jnp.mean(whole * whole, axis=-1, keepdims=True) + 1e-05)
    normed = (whole * inverse * norm_gain.astype(jnp.float32)).astype(jnp.bfloat16)
    gate = jax.nn.sigmoid(jnp.dot(full_rows, router_weight, preferred_element_type=jnp.float32))

    def add_rows(piece):
        return jnp.dot(normed, piece, preferred_element_type=jnp.float32)

    query_raw = add_rows(lax.all_gather(w_query, "seq", axis=0, tiled=True))
    key_raw = add_rows(lax.all_gather(w_key, "seq", axis=0, tiled=True))
    value_raw = add_rows(lax.all_gather(w_value, "seq", axis=0, tiled=True))
    heads = w_query.shape[1] // HEAD_DIM
    query = rotate(query_raw.reshape(sel_rows, heads, HEAD_DIM), picked).astype(jnp.bfloat16)
    keys = rotate(key_raw.reshape(sel_rows, heads, HEAD_DIM), picked).astype(jnp.bfloat16)
    values = value_raw.reshape(sel_rows, heads, HEAD_DIM).astype(jnp.bfloat16)
    rank_q = slots * shards + here
    scale = 1.0 / math.sqrt(HEAD_DIM)
    top = jnp.full((heads, sel_rows), -1e30, jnp.float32)
    piece_k = lax.all_gather(keys, "seq", axis=0, tiled=True)
    piece_v = lax.all_gather(values, "seq", axis=0, tiled=True)
    index = jnp.arange(piece_k.shape[0], dtype=jnp.int32)
    rank_k = index % sel_rows * shards + index // sel_rows
    allowed = (rank_k[None, :] <= rank_q[:, None])[None]
    scores = jnp.einsum("qhd,khd->hqk", query, piece_k, preferred_element_type=jnp.float32) * scale
    scores = jnp.where(allowed, scores, -1e30)
    newtop = jnp.maximum(top, jnp.max(scores, axis=-1))
    weights = jnp.where(allowed, jnp.exp(scores - newtop[..., None]), 0.0)
    total = jnp.sum(weights, axis=-1)
    summed = jnp.einsum(
        "hqk,khd->hqd", weights.astype(jnp.bfloat16), piece_v, preferred_element_type=jnp.float32
    )
    top, total, summed = (newtop, total, summed)
    attended = (
        jnp.transpose(summed / total[..., None], (1, 0, 2))
        .reshape(sel_rows, heads * HEAD_DIM)
        .astype(jnp.bfloat16)
    )
    update = jnp.dot(
        lax.all_gather(attended, "mp", axis=1, tiled=True),
        w_out,
        preferred_element_type=jnp.float32,
    )
    new_rows = (own_rows.astype(jnp.float32) + gate[:, None] * update).astype(jnp.bfloat16)
    backward = jnp.zeros((shards * bucket, part_width), jnp.bfloat16).at[fetch].set(new_rows)
    returned = lax.all_to_all(
        backward.reshape(shards, bucket, part_width), "seq", split_axis=0, concat_axis=0, tiled=True
    )
    taken = returned.reshape(shards * bucket, part_width)[jnp.where(live, cell, 0)]
    return jnp.where(live[:, None], taken, hidden)


def slots_of(target, half):
    live = target >= 0
    rank = (target % 128) * 8 + target // 128
    first = jnp.min(jnp.where(live, rank, 1 << 20), axis=1, keepdims=True)
    parity = rank % 2
    index = rank // 2
    slot = parity * half + index - (first - parity + 1) // 2
    return jnp.where(live, slot, -1), index


def one_hot(row, count):
    return (lax.broadcasted_iota(jnp.int32, (count, row.shape[1]), 0) == row).astype(BF)


def mix_kernel(
    target_ref, hidden_ref, gain_ref, router_ref, wq_ref, wk_ref, wv_ref,
    rows_out, gate_out, att_out,
    stats, nsend, aux, xbuf, auxbuf, pick, dense, ysend, yrecv, zsend, zown, zrecv,
    qbuf, kbuf, vbuf, att, msg, arecv, cosine, sine,
    st_send, st_recv, x_send, x_recv, a_send, a_recv, fx_send, fa_send,
    y_send, y_recv, z_send, z_recv, kv_send, kv_recv, m_send, m_recv,
):
    s = lax.axis_index("seq")
    m = lax.axis_index("mp")
    z, y = s // 2, s % 2
    x, c = m // 2, m % 2
    me = s * 4 + m
    weights = (wk_ref, wv_ref, wq_ref)

    def at(seq, mp):
        return {"seq": seq, "mp": mp}

    def remote(src, dst, send, recv, seq, mp):
        return pltpu.make_async_remote_copy(
            src_ref=src, dst_ref=dst, send_sem=send, recv_sem=recv,
            device_id=at(seq, mp), device_id_type=MESH,
        )

    barrier = pltpu.get_barrier_semaphore()

    @pl.loop(1, 32)
    def _(step):
        other = lax.rem(me + step, 32)
        pl.semaphore_signal(barrier, inc=1, device_id=at(other // 4, other % 4), device_id_type=MESH)

    slot, index = slots_of(target_ref[...], 128)
    chosen = one_hot(slot, 256)
    rows = jnp.dot(chosen, hidden_ref[...], preferred_element_type=F32)
    rows_out[...] = rows.astype(BF)
    squares = jnp.sum(rows * rows, axis=1, keepdims=True)
    logit = jnp.sum(rows * router_ref[pl.ds(m, 1), :], axis=1, keepdims=True)
    lane = lax.broadcasted_iota(jnp.int32, (256, 128), 1)
    table = jnp.where(lane == 0, squares, jnp.where(lane == 1, logit, 0.0))
    stats[m] = table.T[0:8]
    sub = lax.broadcasted_iota(jnp.int32, (8, 1024), 0)
    place = lax.broadcasted_iota(jnp.int32, (8, 1024), 1)
    parts = jnp.where(sub == 0, index // 16, jnp.where(sub == 1, index % 16, jnp.where(
        sub == 2, place // 32, jnp.where(sub == 3, place % 32, 1))))
    parts = lax.dot_general(
        parts.astype(F32).astype(BF), chosen, (((1,), (1,)), ((), ())), preferred_element_type=F32)
    mine = jnp.where(parts[4:5] > 0.5, parts[0:1] * 16.0 + parts[1:2], -1.0)
    spot = parts[2:3] * 32.0 + parts[3:4] + (s * 1024).astype(F32)
    aux[...] = jnp.where(lax.broadcasted_iota(jnp.int32, (8, 256), 0) == 0, mine, spot)

    pl.semaphore_wait(barrier, 31)
    for step in range(1, 4):
        other = lax.rem(m + step, 4)
        remote(stats.at[m], stats.at[m], st_send.at[step - 1], st_recv.at[m], s, other).start()
    for step in range(1, 4):
        other = lax.rem(m + step, 4)
        copy = remote(stats.at[other], stats.at[other], st_send.at[step - 1], st_recv.at[other], s, other)
        copy.wait_recv()
    total = stats[0] + stats[1] + stats[2] + stats[3]
    total = jnp.concatenate([total] * 16, axis=0).T
    gate_out[...] = jnp.broadcast_to(1.0 / (1.0 + jnp.exp(-total[:, 1:2])), (256, 128))
    inverse = lax.rsqrt(total[:, 0:1] * (1.0 / 4096) + 1e-05)
    normed = (rows * inverse * gain_ref[pl.ds(m, 1), :]).astype(BF)
    for half in range(2):
        nsend[half] = normed[:, half * 512:half * 512 + 512].reshape(2, 128, 512)

    here = pl.ds(pl.multiple_of(s * 128, 128), 128)
    for half in range(2):
        for across in range(2):
            number = half * 2 + across
            seq, mp = 2 * m + half, c + 2 * across
            own = jnp.logical_and(seq == s, mp == m)

            @pl.when(own)
            def _():
                xbuf[:, here, :] = nsend[half]
                auxbuf[s] = aux[...]

            @pl.when(jnp.logical_not(own))
            def _():
                remote(nsend.at[half], xbuf.at[:, here, :], x_send.at[number], x_recv.at[s], seq, mp).start()
                remote(aux, auxbuf.at[s], a_send.at[number], a_recv.at[s], seq, mp).start()

    direct = c == z % 2
    sibling = m + 1 - 2 * c

    @pl.loop(0, 8)
    def _(step):
        block = lax.rem(s + step, 8)
        there = pl.ds(pl.multiple_of(block * 128, 128), 128)
        pair = (
            remote(xbuf.at[:, there, :], xbuf.at[:, there, :], fx_send.at[block], x_recv.at[block], s, sibling),
            remote(auxbuf.at[block], auxbuf.at[block], fa_send.at[block], a_recv.at[block], s, sibling),
        )

        @pl.when(jnp.logical_not(jnp.logical_and(m == z, block == s)))
        def _():
            for copy in pair:
                copy.wait_recv()

        @pl.when(direct)
        def _():
            for copy in pair:
                copy.start()

    for parity in range(2):
        line = jnp.concatenate(
            [auxbuf[b][0:1, parity * 128:parity * 128 + 128] for b in range(8)], axis=1).astype(jnp.int32)

        @pl.loop(0, 4)
        def _(tile):
            rows_here = pl.ds(pl.multiple_of(tile * 128, 128), 128)
            hot = (lax.broadcasted_iota(jnp.int32, (128, 1024), 0) + tile * 128 == line).astype(BF)
            pick[parity, rows_here, :] = hot
            dense[parity, rows_here, :] = jnp.dot(
                hot, xbuf[parity], preferred_element_type=F32).astype(BF)

    other_y = 1 - y
    near = s + 1 - 2 * y

    def ycopy(kind):
        return remote(ysend.at[kind], yrecv.at[kind], y_send.at[kind], y_recv.at[kind], near, m)

    def zcopy(kind, step):
        peer = lax.rem(z + step, 4)
        return remote(zsend.at[kind, peer], zrecv.at[kind, z], z_send.at[kind, peer], z_recv.at[kind, z], 2 * peer + y, m)

    def zwait(kind, step):
        peer = lax.rem(z + step, 4)
        remote(zsend.at[kind, peer], zrecv.at[kind, peer], z_send.at[kind, peer], z_recv.at[kind, peer], 2 * peer + y, m).wait_recv()

    for kind in range(3):
        @pl.loop(0, 2)
        def _(tile):
            part = pl.ds(pl.multiple_of(tile * 256, 256), 256)
            ysend[kind, part, :] = jnp.dot(
                dense[other_y, part, :], weights[kind][...], preferred_element_type=F32).astype(BF)

        ycopy(kind).start()

    places = jnp.concatenate([
        jnp.where(y == 0, auxbuf[b][1:2, 0:128], auxbuf[b][1:2, 128:256]) for b in range(8)], axis=1)
    lanes = lax.broadcasted_iota(jnp.int32, (1, 128), 1) % 64
    freq = jnp.exp(-math.log(10000.0) * (2.0 * lanes.astype(F32) / 128))
    sign = jnp.where(lax.broadcasted_iota(jnp.int32, (1, 128), 1) < 64, -1.0, 1.0)

    @pl.loop(0, 4)
    def _(tile):
        part = pl.ds(pl.multiple_of(tile * 128, 128), 128)
        where = jnp.sum(pick[y, part, :].astype(F32) * places, axis=1, keepdims=True)
        angle = where * freq
        cosine[part, :] = jnp.cos(angle)
        sine[part, :] = jnp.sin(angle) * sign

    for kind in range(3):
        ycopy(kind).wait_recv()

        @pl.loop(0, 2)
        def _(tile):
            part = pl.ds(pl.multiple_of(tile * 256, 256), 256)
            value = jnp.dot(dense[y, part, :], weights[kind][...], preferred_element_type=F32)
            value = value + yrecv[kind, part, :].astype(F32)
            for head in range(4):
                zsend[kind, head, part, :] = value[:, head * 128:head * 128 + 128].astype(BF)

        for step in range(1, 4):
            zcopy(kind, step).start()

    def kvcopy(buf, kind):
        return remote(buf.at[y], buf.at[y], kv_send.at[kind], kv_recv.at[kind], near, m)

    for kind in range(3):
        for step in range(1, 4):
            zwait(kind, step)
        value = zsend[kind, z].astype(F32)
        for step in range(1, 4):
            value = value + zrecv[kind, lax.rem(z + step, 4)].astype(F32)
        if kind != 1:
            value = value * cosine[...] + pltpu.roll(value, 64, 1) * sine[...]
        if kind == 2:
            qbuf[...] = value.astype(BF)
        else:
            buf = (kbuf, vbuf)[kind]
            buf[y] = value.astype(BF)
            kvcopy(buf, kind).start()
    for kind, buf in enumerate((kbuf, vbuf)):
        remote(buf.at[other_y], buf.at[other_y], kv_send.at[kind], kv_recv.at[kind], near, m).wait_recv()

    @pl.loop(0, 4)
    def _(tile):
        part = pl.ds(pl.multiple_of(tile * 128, 128), 128)
        keys = kbuf[...].reshape(1024, 128)
        scores = lax.dot_general(
            qbuf[part, :], keys, (((1,), (1,)), ((), ())), preferred_element_type=F32) * (1.0 / math.sqrt(HEAD_DIM))
        column = lax.broadcasted_iota(jnp.int32, (128, 1024), 1)
        rank_k = 2 * (column % 512) + column // 512
        rank_q = 2 * (lax.broadcasted_iota(jnp.int32, (128, 1024), 0) + tile * 128) + y
        allowed = rank_k <= rank_q
        scores = jnp.where(allowed, scores, -1e30)
        top = jnp.max(scores, axis=1, keepdims=True)
        weight = jnp.where(allowed, jnp.exp(scores - top), 0.0)
        total = jnp.sum(weight, axis=1, keepdims=True)
        summed = jnp.dot(weight.astype(BF), vbuf[...].reshape(1024, 128), preferred_element_type=F32)
        att[part, :] = (summed / total).astype(BF)

    messages = lax.dot_general(
        pick[y], att[...], (((0,), (0,)), ((), ())), preferred_element_type=F32)
    msg[...] = messages.astype(BF).reshape(8, 128, 128)
    part = pl.ds(pl.multiple_of(y * 128, 128), 128)
    head = m * 4 + z
    column = pl.ds(pl.multiple_of(head * 128, 128), 128)
    arecv[part, column] = msg[s]

    def mcopy(step):
        other = lax.rem(me + step, 32)
        return remote(msg.at[other // 4], arecv.at[part, column], m_send.at[other], m_recv.at[me], other // 4, other % 4)

    @pl.loop(1, 32)
    def _(step):
        mcopy(step).start()

    @pl.loop(1, 32)
    def _(step):
        other = lax.rem(me + step, 32)
        seq, mp = other // 4, other % 4
        to_part = pl.ds(pl.multiple_of(seq % 2 * 128, 128), 128)
        to_column = pl.ds(pl.multiple_of((mp * 4 + seq // 2) * 128, 128), 128)
        remote(msg.at[seq], arecv.at[to_part, to_column], m_send.at[other], m_recv.at[other], seq, mp).wait_recv()

    att_out[...] = arecv[...]

    for step in range(1, 4):
        other = lax.rem(m + step, 4)
        remote(stats.at[m], stats.at[m], st_send.at[step - 1], st_recv.at[m], s, other).wait_send()
    for half in range(2):
        for across in range(2):
            number = half * 2 + across
            seq, mp = 2 * m + half, c + 2 * across

            @pl.when(jnp.logical_not(jnp.logical_and(seq == s, mp == m)))
            def _():
                remote(nsend.at[half], xbuf.at[:, here, :], x_send.at[number], x_recv.at[s], seq, mp).wait_send()
                remote(aux, auxbuf.at[s], a_send.at[number], a_recv.at[s], seq, mp).wait_send()

    @pl.when(direct)
    def _():
        @pl.loop(0, 8)
        def _(block):
            there = pl.ds(pl.multiple_of(block * 128, 128), 128)
            remote(xbuf.at[:, there, :], xbuf.at[:, there, :], fx_send.at[block], x_recv.at[block], s, sibling).wait_send()
            remote(auxbuf.at[block], auxbuf.at[block], fa_send.at[block], a_recv.at[block], s, sibling).wait_send()

    for kind in range(3):
        ycopy(kind).wait_send()
        for step in range(1, 4):
            zcopy(kind, step).wait_send()
    for kind, buf in enumerate((kbuf, vbuf)):
        kvcopy(buf, kind).wait_send()

    @pl.loop(1, 32)
    def _(step):
        mcopy(step).wait_send()


def finish_kernel(target_ref, hidden_ref, rows_ref, gate_ref, att_ref, w_out_ref, mixed_ref):
    slot, _ = slots_of(target_ref[...], 128)
    chosen = one_hot(slot, 256)
    flags = lax.dot_general(
        chosen, jnp.ones((256, 128), BF), (((0,), (0,)), ((), ())), preferred_element_type=F32)
    update = jnp.dot(att_ref[...], w_out_ref[...], preferred_element_type=F32)
    fresh = (rows_ref[...].astype(F32) + gate_ref[:, 0:1] * update).astype(BF)
    spread = lax.dot_general(chosen, fresh, (((0,), (0,)), ((), ())), preferred_element_type=F32)
    mixed_ref[...] = jnp.where(flags[:, 0:1] > 0.5, spread, hidden_ref[...].astype(F32)).astype(BF)


def fused(hidden, picked, target, norm_gain, router_weight, w_query, w_key, w_value, w_out):
    target = target.reshape(1, 1024)
    gain = norm_gain.reshape(4, 1024).astype(F32)
    router = router_weight.reshape(4, 1024).astype(F32)
    dma = pltpu.SemaphoreType.DMA
    rows, gate, att = pl.pallas_call(
        mix_kernel,
        out_shape=(
            jax.ShapeDtypeStruct((256, 1024), BF),
            jax.ShapeDtypeStruct((256, 128), F32),
            jax.ShapeDtypeStruct((256, 2048), BF),
        ),
        in_specs=[pl.BlockSpec(memory_space=pltpu.VMEM)] * 7,
        out_specs=[pl.BlockSpec(memory_space=pltpu.VMEM)] * 3,
        scratch_shapes=[
            pltpu.VMEM((4, 8, 256), F32),
            pltpu.VMEM((2, 2, 128, 512), BF),
            pltpu.VMEM((8, 256), F32),
            pltpu.VMEM((2, 1024, 512), BF),
            pltpu.VMEM((8, 8, 256), F32),
            pltpu.VMEM((2, 512, 1024), BF),
            pltpu.VMEM((2, 512, 512), BF),
            pltpu.VMEM((3, 512, 512), BF),
            pltpu.VMEM((3, 512, 512), BF),
            pltpu.VMEM((3, 4, 512, 128), BF),
            pltpu.VMEM((8, 128), F32),
            pltpu.VMEM((3, 4, 512, 128), BF),
            pltpu.VMEM((512, 128), BF),
            pltpu.VMEM((2, 512, 128), BF),
            pltpu.VMEM((2, 512, 128), BF),
            pltpu.VMEM((512, 128), BF),
            pltpu.VMEM((8, 128, 128), BF),
            pltpu.VMEM((256, 2048), BF),
            pltpu.VMEM((512, 128), F32),
            pltpu.VMEM((512, 128), F32),
            dma((3,)), dma((4,)), dma((4,)), dma((8,)), dma((4,)), dma((8,)), dma((8,)), dma((8,)),
            dma((3,)), dma((3,)), dma((3, 4)), dma((3, 4)), dma((2,)), dma((2,)), dma((32,)), dma((32,)),
        ],
        compiler_params=pltpu.CompilerParams(
            collective_id=0, has_side_effects=True, vmem_limit_bytes=48 * 2 ** 20),
    )(target, hidden, gain, router, w_query, w_key, w_value)
    return pl.pallas_call(
        finish_kernel,
        out_shape=jax.ShapeDtypeStruct((1024, 1024), BF),
        in_specs=[pl.BlockSpec(memory_space=pltpu.VMEM)] * 6,
        out_specs=pl.BlockSpec(memory_space=pltpu.VMEM),
        compiler_params=pltpu.CompilerParams(vmem_limit_bytes=48 * 2 ** 20),
    )(target, hidden, rows, gate, att, w_out)


def per_device(hidden, picked, target, *rest):
    small = (
        lax.axis_size("seq") == 8 and lax.axis_size("mp") == 4
        and hidden.shape == (1024, 1024) and picked.shape[0] == 128
    )
    return (fused if small else general)(hidden, picked, target, *rest)


def solution(mesh):
    placed = (
        P("seq", "mp"),
        P("seq"),
        P("seq"),
        P(),
        P(),
        P("seq", "mp"),
        P("seq", "mp"),
        P("seq", "mp"),
        P(None, "mp"),
    )
    return jax.shard_map(
        per_device, mesh=mesh, in_specs=placed, out_specs=P("seq", "mp"), check_vma=False
    )
```

```python
import math

import jax
import jax.numpy as jnp
from jax import lax
from jax.experimental import pallas as pl
from jax.experimental.pallas import tpu as pltpu
from jax.sharding import PartitionSpec as P

HEAD_DIM = 128
MESH = pl.DeviceIdType.MESH
BF = jnp.bfloat16
F32 = jnp.float32


def rotate(vec, positions):
    half = vec.shape[-1] // 2
    freq = jnp.exp(-math.log(10000.0) * (2.0 * jnp.arange(half, dtype=jnp.float32) / vec.shape[-1]))
    angle = positions.astype(jnp.float32)[:, None] * freq[None, :]
    cosine = jnp.cos(angle)[:, None, :]
    sine = jnp.sin(angle)[:, None, :]
    first = vec[..., :half]
    second = vec[..., half:]
    return jnp.concatenate(
        [first * cosine - second * sine, second * cosine + first * sine], axis=-1
    )


def general(hidden, picked, target, norm_gain, router_weight, w_query, w_key, w_value, w_out):
    shards = lax.axis_size("seq")
    here = lax.axis_index("seq")
    tok_rows = hidden.shape[0]
    part_width = hidden.shape[1]
    sel_rows = picked.shape[0]
    bucket = (2 * sel_rows + shards - 1) // shards
    live = target >= 0
    dest = jnp.where(live, target // sel_rows, shards)
    cell = dest * bucket + jnp.where(live, target % sel_rows, 0) % bucket
    table = jnp.full((shards * bucket,), tok_rows, jnp.int32)
    table = table.at[cell].set(jnp.arange(tok_rows, dtype=jnp.int32), mode="drop")
    padded = jnp.concatenate([hidden, jnp.zeros((1, part_width), hidden.dtype)], axis=0)
    outgoing = padded[table].reshape(shards, bucket, part_width)
    slots = jnp.arange(sel_rows, dtype=jnp.int32)
    source = picked // tok_rows
    fetch = source * bucket + slots % bucket
    arrived = lax.all_to_all(outgoing, "seq", split_axis=0, concat_axis=0, tiled=True)
    own_rows = arrived.reshape(shards * bucket, part_width)[fetch]
    full_rows = lax.all_gather(own_rows, "mp", axis=1, tiled=True)
    whole = full_rows.astype(jnp.float32)
    inverse = lax.rsqrt(jnp.mean(whole * whole, axis=-1, keepdims=True) + 1e-05)
    normed = (whole * inverse * norm_gain.astype(jnp.float32)).astype(jnp.bfloat16)
    gate = jax.nn.sigmoid(jnp.dot(full_rows, router_weight, preferred_element_type=jnp.float32))

    def add_rows(piece):
        return jnp.dot(normed, piece, preferred_element_type=jnp.float32)

    query_raw = add_rows(lax.all_gather(w_query, "seq", axis=0, tiled=True))
    key_raw = add_rows(lax.all_gather(w_key, "seq", axis=0, tiled=True))
    value_raw = add_rows(lax.all_gather(w_value, "seq", axis=0, tiled=True))
    heads = w_query.shape[1] // HEAD_DIM
    query = rotate(query_raw.reshape(sel_rows, heads, HEAD_DIM), picked).astype(jnp.bfloat16)
    keys = rotate(key_raw.reshape(sel_rows, heads, HEAD_DIM), picked).astype(jnp.bfloat16)
    values = value_raw.reshape(sel_rows, heads, HEAD_DIM).astype(jnp.bfloat16)
    rank_q = slots * shards + here
    scale = 1.0 / math.sqrt(HEAD_DIM)
    top = jnp.full((heads, sel_rows), -1e30, jnp.float32)
    piece_k = lax.all_gather(keys, "seq", axis=0, tiled=True)
    piece_v = lax.all_gather(values, "seq", axis=0, tiled=True)
    index = jnp.arange(piece_k.shape[0], dtype=jnp.int32)
    rank_k = index % sel_rows * shards + index // sel_rows
    allowed = (rank_k[None, :] <= rank_q[:, None])[None]
    scores = jnp.einsum("qhd,khd->hqk", query, piece_k, preferred_element_type=jnp.float32) * scale
    scores = jnp.where(allowed, scores, -1e30)
    newtop = jnp.maximum(top, jnp.max(scores, axis=-1))
    weights = jnp.where(allowed, jnp.exp(scores - newtop[..., None]), 0.0)
    total = jnp.sum(weights, axis=-1)
    summed = jnp.einsum(
        "hqk,khd->hqd", weights.astype(jnp.bfloat16), piece_v, preferred_element_type=jnp.float32
    )
    top, total, summed = (newtop, total, summed)
    attended = (
        jnp.transpose(summed / total[..., None], (1, 0, 2))
        .reshape(sel_rows, heads * HEAD_DIM)
        .astype(jnp.bfloat16)
    )
    update = jnp.dot(
        lax.all_gather(attended, "mp", axis=1, tiled=True),
        w_out,
        preferred_element_type=jnp.float32,
    )
    new_rows = (own_rows.astype(jnp.float32) + gate[:, None] * update).astype(jnp.bfloat16)
    backward = jnp.zeros((shards * bucket, part_width), jnp.bfloat16).at[fetch].set(new_rows)
    returned = lax.all_to_all(
        backward.reshape(shards, bucket, part_width), "seq", split_axis=0, concat_axis=0, tiled=True
    )
    taken = returned.reshape(shards * bucket, part_width)[jnp.where(live, cell, 0)]
    return jnp.where(live[:, None], taken, hidden)


def slots_of(target, half):
    live = target >= 0
    rank = (target % 128) * 8 + target // 128
    first = jnp.min(jnp.where(live, rank, 1 << 20), axis=1, keepdims=True)
    parity = rank % 2
    index = rank // 2
    slot = parity * half + index - (first - parity + 1) // 2
    return jnp.where(live, slot, -1), index


def one_hot(row, count):
    return (lax.broadcasted_iota(jnp.int32, (count, row.shape[1]), 0) == row).astype(BF)


def mix_kernel(
    target_ref, hidden_hbm, gain_ref, router_ref, wq_ref, wk_ref, wv_ref,
    rows_out, gate_out, att_out,
    hidden_ref, wbuf, stats, nsend, aux, xbuf, auxbuf, pick, dense, zsend, zrecv,
    qbuf, kbuf, vbuf, att, msg, arecv, cosine, sine,
    h_sem, w_sem, w_send, w_recv,
    st_send, st_recv, x_send, x_recv, a_send, a_recv, fx_send, fa_send, gx_send, ga_send,
    z_send, z_recv, kv_send, kv_recv, m_send, m_recv,
):
    s = lax.axis_index("seq")
    m = lax.axis_index("mp")
    z, y = s // 2, s % 2
    x, c = m // 2, m % 2
    me = s * 4 + m
    weights = (wk_ref, wv_ref, wq_ref)

    def at(seq, mp):
        return {"seq": seq, "mp": mp}

    def remote(src, dst, send, recv, seq, mp):
        return pltpu.make_async_remote_copy(
            src_ref=src, dst_ref=dst, send_sem=send, recv_sem=recv,
            device_id=at(seq, mp), device_id_type=MESH,
        )

    barrier = pltpu.get_barrier_semaphore()

    @pl.loop(1, 32)
    def _(step):
        other = lax.rem(me + step, 32)
        pl.semaphore_signal(barrier, inc=1, device_id=at(other // 4, other % 4), device_id_type=MESH)

    near = s + 1 - 2 * y
    other_y = 1 - y
    hidden_copy = pltpu.make_async_copy(hidden_hbm, hidden_ref, h_sem)
    hidden_copy.start()

    def wcopy(kind):
        return remote(weights[kind], wbuf.at[kind, y], w_send.at[kind], w_recv.at[kind], near, m)

    def wlocal(kind):
        return pltpu.make_async_copy(weights[kind], wbuf.at[kind, y], w_sem.at[kind])

    pl.semaphore_wait(barrier, 31)
    for kind in range(3):
        wcopy(kind).start()
    for kind in range(3):
        wlocal(kind).start()
    hidden_copy.wait()

    slot, index = slots_of(target_ref[...], 128)
    chosen = one_hot(slot, 256)
    rows = jnp.dot(chosen, hidden_ref[...], preferred_element_type=F32)
    rows_out[...] = rows.astype(BF)
    squares = jnp.sum(rows * rows, axis=1, keepdims=True)
    logit = jnp.sum(rows * router_ref[pl.ds(m, 1), :], axis=1, keepdims=True)
    lane = lax.broadcasted_iota(jnp.int32, (256, 128), 1)
    table = jnp.where(lane == 0, squares, jnp.where(lane == 1, logit, 0.0))
    stats[m] = table.T[0:8]
    sub = lax.broadcasted_iota(jnp.int32, (8, 1024), 0)
    place = lax.broadcasted_iota(jnp.int32, (8, 1024), 1)
    parts = jnp.where(sub == 0, index // 16, jnp.where(sub == 1, index % 16, jnp.where(
        sub == 2, place // 32, jnp.where(sub == 3, place % 32, 1))))
    parts = lax.dot_general(
        parts.astype(F32).astype(BF), chosen, (((1,), (1,)), ((), ())), preferred_element_type=F32)
    mine = jnp.where(parts[4:5] > 0.5, parts[0:1] * 16.0 + parts[1:2], -1.0)
    spot = parts[2:3] * 32.0 + parts[3:4] + (s * 1024).astype(F32)
    aux[...] = jnp.where(lax.broadcasted_iota(jnp.int32, (8, 256), 0) == 0, mine, spot)

    for step in range(1, 4):
        other = lax.rem(m + step, 4)
        remote(stats.at[m], stats.at[m], st_send.at[step - 1], st_recv.at[m], s, other).start()
    for step in range(1, 4):
        other = lax.rem(m + step, 4)
        copy = remote(stats.at[other], stats.at[other], st_send.at[step - 1], st_recv.at[other], s, other)
        copy.wait_recv()
    total = stats[0] + stats[1] + stats[2] + stats[3]
    total = jnp.concatenate([total] * 16, axis=0).T
    gate_out[...] = jnp.broadcast_to(1.0 / (1.0 + jnp.exp(-total[:, 1:2])), (256, 128))
    inverse = lax.rsqrt(total[:, 0:1] * (1.0 / 4096) + 1e-05)
    nsend[...] = (rows * inverse * gain_ref[pl.ds(m, 1), :]).astype(BF)

    here = pl.ds(pl.multiple_of(s * 128, 128), 128)

    def xcopies(half):
        seq, mp = 2 * m + half, c + 2 * lax.rem(y + half, 2)
        own = jnp.logical_and(seq == s, mp == m)
        return own, (
            remote(nsend.at[pl.ds(half * 128, 128), :], xbuf.at[here, :], x_send.at[half], x_recv.at[s], seq, mp),
            remote(aux, auxbuf.at[s], a_send.at[half], a_recv.at[s], seq, mp),
        )

    for half in range(2):
        own, pair = xcopies(half)

        @pl.when(own)
        def _():
            xbuf[here, :] = nsend[half * 128:half * 128 + 128, :]
            auxbuf[s] = aux[...]

        @pl.when(jnp.logical_not(own))
        def _():
            for copy in pair:
                copy.start()

    direct = c == z % 2

    def forward(step, to_core):
        landing = lax.rem(x + y + step // 4, 2)
        block = 2 * lax.rem(z + step, 4) + landing
        there = pl.ds(pl.multiple_of(block * 128, 128), 128)
        mp = m + 1 - 2 * c if to_core else lax.rem(m + 2, 4)
        x_sems, a_sems = (fx_send, fa_send) if to_core else (gx_send, ga_send)
        return block, (
            remote(xbuf.at[there, :], xbuf.at[there, :], x_sems.at[block], x_recv.at[block], s, mp),
            remote(auxbuf.at[block], auxbuf.at[block], a_sems.at[block], a_recv.at[block], s, mp),
        )

    @pl.loop(0, 8)
    def _(step):
        block, pair = forward(step, True)
        _, across = forward(step, False)

        @pl.when(jnp.logical_not(jnp.logical_and(jnp.logical_and(m == z, x == 0), block == s)))
        def _():
            for copy in pair:
                copy.wait_recv()

        @pl.when(jnp.logical_and(direct, step < 4))
        def _():
            for copy in across:
                copy.start()

        @pl.when(direct)
        def _():
            for copy in pair:
                copy.start()

    def line_of(which):
        return jnp.concatenate([jnp.where(
            y == 0, auxbuf[b][which:which + 1, 0:128], auxbuf[b][which:which + 1, 128:256]) for b in range(8)], axis=1)

    line = line_of(0).astype(jnp.int32)

    @pl.loop(0, 4)
    def _(tile):
        part = pl.ds(pl.multiple_of(tile * 128, 128), 128)
        hot = (lax.broadcasted_iota(jnp.int32, (128, 1024), 0) + tile * 128 == line).astype(BF)
        pick[part, :] = hot
        dense[part, :] = jnp.dot(hot, xbuf[...], preferred_element_type=F32).astype(BF)

    def zcopy(kind, step):
        peer = lax.rem(z + step, 4)
        return remote(zsend.at[kind, peer], zrecv.at[kind, z], z_send.at[kind, peer], z_recv.at[kind, z], 2 * peer + y, m)

    def zwait(kind, step):
        peer = lax.rem(z + step, 4)
        remote(zsend.at[kind, peer], zrecv.at[kind, peer], z_send.at[kind, peer], z_recv.at[kind, peer], 2 * peer + y, m).wait_recv()

    for kind in range(3):
        wlocal(kind).wait()
        remote(weights[kind], wbuf.at[kind, other_y], w_send.at[kind], w_recv.at[kind], near, m).wait_recv()

        @pl.loop(0, 2)
        def _(tile):
            part = pl.ds(pl.multiple_of(tile * 256, 256), 256)
            value = jnp.dot(
                dense[part, :], wbuf[kind].reshape(1024, 512), preferred_element_type=F32).astype(BF)
            for head in range(4):
                zsend[kind, head, part, :] = value[:, head * 128:head * 128 + 128]

        for step in range(1, 4):
            zcopy(kind, step).start()

    places = line_of(1)
    lanes = lax.broadcasted_iota(jnp.int32, (1, 128), 1) % 64
    freq = jnp.exp(-math.log(10000.0) * (2.0 * lanes.astype(F32) / 128))
    sign = jnp.where(lax.broadcasted_iota(jnp.int32, (1, 128), 1) < 64, -1.0, 1.0)

    @pl.loop(0, 4)
    def _(tile):
        part = pl.ds(pl.multiple_of(tile * 128, 128), 128)
        where = jnp.sum(pick[part, :].astype(F32) * places, axis=1, keepdims=True)
        angle = where * freq
        cosine[part, :] = jnp.cos(angle)
        sine[part, :] = jnp.sin(angle) * sign

    def kvcopy(buf, kind):
        return remote(buf.at[y], buf.at[y], kv_send.at[kind], kv_recv.at[kind], near, m)

    for kind in range(3):
        for step in range(1, 4):
            zwait(kind, step)
        value = zsend[kind, z].astype(F32)
        for step in range(1, 4):
            value = value + zrecv[kind, lax.rem(z + step, 4)].astype(F32)
        if kind != 1:
            value = value * cosine[...] + pltpu.roll(value, 64, 1) * sine[...]
        if kind == 2:
            qbuf[...] = value.astype(BF)
        else:
            buf = (kbuf, vbuf)[kind]
            buf[y] = value.astype(BF)
            kvcopy(buf, kind).start()
    for kind, buf in enumerate((kbuf, vbuf)):
        remote(buf.at[other_y], buf.at[other_y], kv_send.at[kind], kv_recv.at[kind], near, m).wait_recv()

    @pl.loop(0, 4)
    def _(tile):
        part = pl.ds(pl.multiple_of(tile * 128, 128), 128)
        keys = kbuf[...].reshape(1024, 128)
        scores = lax.dot_general(
            qbuf[part, :], keys, (((1,), (1,)), ((), ())), preferred_element_type=F32) * (1.0 / math.sqrt(HEAD_DIM))
        column = lax.broadcasted_iota(jnp.int32, (128, 1024), 1)
        rank_k = 2 * (column % 512) + column // 512
        rank_q = 2 * (lax.broadcasted_iota(jnp.int32, (128, 1024), 0) + tile * 128) + y
        allowed = rank_k <= rank_q
        scores = jnp.where(allowed, scores, -1e30)
        top = jnp.max(scores, axis=1, keepdims=True)
        weight = jnp.where(allowed, jnp.exp(scores - top), 0.0)
        total = jnp.sum(weight, axis=1, keepdims=True)
        summed = jnp.dot(weight.astype(BF), vbuf[...].reshape(1024, 128), preferred_element_type=F32)
        att[part, :] = (summed / total).astype(BF)

    messages = lax.dot_general(
        pick[...], att[...], (((0,), (0,)), ((), ())), preferred_element_type=F32)
    msg[...] = messages.astype(BF).reshape(8, 128, 128)
    part = pl.ds(pl.multiple_of(y * 128, 128), 128)
    head = m * 4 + z
    column = pl.ds(pl.multiple_of(head * 128, 128), 128)
    arecv[part, column] = msg[s]

    def mcopy(step):
        other = lax.rem(me + step, 32)
        return remote(msg.at[other // 4], arecv.at[part, column], m_send.at[other], m_recv.at[me], other // 4, other % 4)

    @pl.loop(1, 32)
    def _(step):
        mcopy(step).start()

    @pl.loop(1, 32)
    def _(step):
        other = lax.rem(me + step, 32)
        seq, mp = other // 4, other % 4
        to_part = pl.ds(pl.multiple_of(seq % 2 * 128, 128), 128)
        to_column = pl.ds(pl.multiple_of((mp * 4 + seq // 2) * 128, 128), 128)
        remote(msg.at[seq], arecv.at[to_part, to_column], m_send.at[other], m_recv.at[other], seq, mp).wait_recv()

    att_out[...] = arecv[...]

    for step in range(1, 4):
        other = lax.rem(m + step, 4)
        remote(stats.at[m], stats.at[m], st_send.at[step - 1], st_recv.at[m], s, other).wait_send()
    for half in range(2):
        own, pair = xcopies(half)

        @pl.when(jnp.logical_not(own))
        def _():
            for copy in pair:
                copy.wait_send()

    @pl.when(direct)
    def _():
        @pl.loop(0, 8)
        def _(step):
            for copy in forward(step, True)[1]:
                copy.wait_send()

            @pl.when(step < 4)
            def _():
                for copy in forward(step, False)[1]:
                    copy.wait_send()

    for kind in range(3):
        wcopy(kind).wait_send()
        for step in range(1, 4):
            zcopy(kind, step).wait_send()
    for kind, buf in enumerate((kbuf, vbuf)):
        kvcopy(buf, kind).wait_send()

    @pl.loop(1, 32)
    def _(step):
        mcopy(step).wait_send()


def finish_kernel(target_ref, hidden_ref, rows_ref, gate_ref, att_ref, w_out_ref, mixed_ref):
    slot, _ = slots_of(target_ref[...], 128)
    chosen = one_hot(slot, 256)
    flags = lax.dot_general(
        chosen, jnp.ones((256, 128), BF), (((0,), (0,)), ((), ())), preferred_element_type=F32)
    update = jnp.dot(att_ref[...], w_out_ref[...], preferred_element_type=F32)
    fresh = (rows_ref[...].astype(F32) + gate_ref[:, 0:1] * update).astype(BF)
    spread = lax.dot_general(chosen, fresh, (((0,), (0,)), ((), ())), preferred_element_type=F32)
    mixed_ref[...] = jnp.where(flags[:, 0:1] > 0.5, spread, hidden_ref[...].astype(F32)).astype(BF)


def fused(hidden, picked, target, norm_gain, router_weight, w_query, w_key, w_value, w_out):
    target = target.reshape(1, 1024)
    gain = norm_gain.reshape(4, 1024).astype(F32)
    router = router_weight.reshape(4, 1024).astype(F32)
    dma = pltpu.SemaphoreType.DMA
    rows, gate, att = pl.pallas_call(
        mix_kernel,
        out_shape=(
            jax.ShapeDtypeStruct((256, 1024), BF),
            jax.ShapeDtypeStruct((256, 128), F32),
            jax.ShapeDtypeStruct((256, 2048), BF),
        ),
        in_specs=[
            pl.BlockSpec(memory_space=pltpu.VMEM), pl.BlockSpec(memory_space=pl.ANY),
            pl.BlockSpec(memory_space=pltpu.VMEM), pl.BlockSpec(memory_space=pltpu.VMEM),
        ] + [pl.BlockSpec(memory_space=pl.ANY)] * 3,
        out_specs=[pl.BlockSpec(memory_space=pltpu.VMEM)] * 3,
        scratch_shapes=[
            pltpu.VMEM((1024, 1024), BF),
            pltpu.VMEM((3, 2, 512, 512), BF),
            pltpu.VMEM((4, 8, 256), F32),
            pltpu.VMEM((256, 1024), BF),
            pltpu.VMEM((8, 256), F32),
            pltpu.VMEM((1024, 1024), BF),
            pltpu.VMEM((8, 8, 256), F32),
            pltpu.VMEM((512, 1024), BF),
            pltpu.VMEM((512, 1024), BF),
            pltpu.VMEM((3, 4, 512, 128), BF),
            pltpu.VMEM((3, 4, 512, 128), BF),
            pltpu.VMEM((512, 128), BF),
            pltpu.VMEM((2, 512, 128), BF),
            pltpu.VMEM((2, 512, 128), BF),
            pltpu.VMEM((512, 128), BF),
            pltpu.VMEM((8, 128, 128), BF),
            pltpu.VMEM((256, 2048), BF),
            pltpu.VMEM((512, 128), F32),
            pltpu.VMEM((512, 128), F32),
            dma(()), dma((3,)), dma((3,)), dma((3,)),
            dma((3,)), dma((4,)), dma((2,)), dma((8,)), dma((2,)), dma((8,)), dma((8,)), dma((8,)), dma((8,)), dma((8,)),
            dma((3, 4)), dma((3, 4)), dma((2,)), dma((2,)), dma((32,)), dma((32,)),
        ],
        compiler_params=pltpu.CompilerParams(
            collective_id=0, has_side_effects=True, vmem_limit_bytes=48 * 2 ** 20),
    )(target, hidden, gain, router, w_query, w_key, w_value)
    return pl.pallas_call(
        finish_kernel,
        out_shape=jax.ShapeDtypeStruct((1024, 1024), BF),
        in_specs=[pl.BlockSpec(memory_space=pltpu.VMEM)] * 6,
        out_specs=pl.BlockSpec(memory_space=pltpu.VMEM),
        compiler_params=pltpu.CompilerParams(vmem_limit_bytes=48 * 2 ** 20),
    )(target, hidden, rows, gate, att, w_out)


def per_device(hidden, picked, target, *rest):
    small = (
        lax.axis_size("seq") == 8 and lax.axis_size("mp") == 4
        and hidden.shape == (1024, 1024) and picked.shape[0] == 128
    )
    return (fused if small else general)(hidden, picked, target, *rest)


def solution(mesh):
    placed = (
        P("seq", "mp"),
        P("seq"),
        P("seq"),
        P(),
        P(),
        P("seq", "mp"),
        P("seq", "mp"),
        P("seq", "mp"),
        P(None, "mp"),
    )
    return jax.shard_map(
        per_device, mesh=mesh, in_specs=placed, out_specs=P("seq", "mp"), check_vma=False
    )
```

```python
import math

import jax
import jax.numpy as jnp
from jax import lax
from jax.experimental import pallas as pl
from jax.experimental.pallas import tpu as pltpu
from jax.sharding import PartitionSpec as P

HEAD_DIM = 128
MESH = pl.DeviceIdType.MESH
BF = jnp.bfloat16
F32 = jnp.float32


def rotate(vec, positions):
    half = vec.shape[-1] // 2
    freq = jnp.exp(-math.log(10000.0) * (2.0 * jnp.arange(half, dtype=jnp.float32) / vec.shape[-1]))
    angle = positions.astype(jnp.float32)[:, None] * freq[None, :]
    cosine = jnp.cos(angle)[:, None, :]
    sine = jnp.sin(angle)[:, None, :]
    first = vec[..., :half]
    second = vec[..., half:]
    return jnp.concatenate(
        [first * cosine - second * sine, second * cosine + first * sine], axis=-1
    )


def general(hidden, picked, target, norm_gain, router_weight, w_query, w_key, w_value, w_out):
    shards = lax.axis_size("seq")
    here = lax.axis_index("seq")
    tok_rows = hidden.shape[0]
    part_width = hidden.shape[1]
    sel_rows = picked.shape[0]
    bucket = (2 * sel_rows + shards - 1) // shards
    live = target >= 0
    dest = jnp.where(live, target // sel_rows, shards)
    cell = dest * bucket + jnp.where(live, target % sel_rows, 0) % bucket
    table = jnp.full((shards * bucket,), tok_rows, jnp.int32)
    table = table.at[cell].set(jnp.arange(tok_rows, dtype=jnp.int32), mode="drop")
    padded = jnp.concatenate([hidden, jnp.zeros((1, part_width), hidden.dtype)], axis=0)
    outgoing = padded[table].reshape(shards, bucket, part_width)
    slots = jnp.arange(sel_rows, dtype=jnp.int32)
    source = picked // tok_rows
    fetch = source * bucket + slots % bucket
    arrived = lax.all_to_all(outgoing, "seq", split_axis=0, concat_axis=0, tiled=True)
    own_rows = arrived.reshape(shards * bucket, part_width)[fetch]
    full_rows = lax.all_gather(own_rows, "mp", axis=1, tiled=True)
    whole = full_rows.astype(jnp.float32)
    inverse = lax.rsqrt(jnp.mean(whole * whole, axis=-1, keepdims=True) + 1e-05)
    normed = (whole * inverse * norm_gain.astype(jnp.float32)).astype(jnp.bfloat16)
    gate = jax.nn.sigmoid(jnp.dot(full_rows, router_weight, preferred_element_type=jnp.float32))

    def add_rows(piece):
        return jnp.dot(normed, piece, preferred_element_type=jnp.float32)

    query_raw = add_rows(lax.all_gather(w_query, "seq", axis=0, tiled=True))
    key_raw = add_rows(lax.all_gather(w_key, "seq", axis=0, tiled=True))
    value_raw = add_rows(lax.all_gather(w_value, "seq", axis=0, tiled=True))
    heads = w_query.shape[1] // HEAD_DIM
    query = rotate(query_raw.reshape(sel_rows, heads, HEAD_DIM), picked).astype(jnp.bfloat16)
    keys = rotate(key_raw.reshape(sel_rows, heads, HEAD_DIM), picked).astype(jnp.bfloat16)
    values = value_raw.reshape(sel_rows, heads, HEAD_DIM).astype(jnp.bfloat16)
    rank_q = slots * shards + here
    scale = 1.0 / math.sqrt(HEAD_DIM)
    top = jnp.full((heads, sel_rows), -1e30, jnp.float32)
    piece_k = lax.all_gather(keys, "seq", axis=0, tiled=True)
    piece_v = lax.all_gather(values, "seq", axis=0, tiled=True)
    index = jnp.arange(piece_k.shape[0], dtype=jnp.int32)
    rank_k = index % sel_rows * shards + index // sel_rows
    allowed = (rank_k[None, :] <= rank_q[:, None])[None]
    scores = jnp.einsum("qhd,khd->hqk", query, piece_k, preferred_element_type=jnp.float32) * scale
    scores = jnp.where(allowed, scores, -1e30)
    newtop = jnp.maximum(top, jnp.max(scores, axis=-1))
    weights = jnp.where(allowed, jnp.exp(scores - newtop[..., None]), 0.0)
    total = jnp.sum(weights, axis=-1)
    summed = jnp.einsum(
        "hqk,khd->hqd", weights.astype(jnp.bfloat16), piece_v, preferred_element_type=jnp.float32
    )
    top, total, summed = (newtop, total, summed)
    attended = (
        jnp.transpose(summed / total[..., None], (1, 0, 2))
        .reshape(sel_rows, heads * HEAD_DIM)
        .astype(jnp.bfloat16)
    )
    update = jnp.dot(
        lax.all_gather(attended, "mp", axis=1, tiled=True),
        w_out,
        preferred_element_type=jnp.float32,
    )
    new_rows = (own_rows.astype(jnp.float32) + gate[:, None] * update).astype(jnp.bfloat16)
    backward = jnp.zeros((shards * bucket, part_width), jnp.bfloat16).at[fetch].set(new_rows)
    returned = lax.all_to_all(
        backward.reshape(shards, bucket, part_width), "seq", split_axis=0, concat_axis=0, tiled=True
    )
    taken = returned.reshape(shards * bucket, part_width)[jnp.where(live, cell, 0)]
    return jnp.where(live[:, None], taken, hidden)


def slots_of(target, half):
    live = target >= 0
    rank = (target % 128) * 8 + target // 128
    first = jnp.min(jnp.where(live, rank, 1 << 20), axis=1, keepdims=True)
    parity = rank % 2
    index = rank // 2
    slot = parity * half + index - (first - parity + 1) // 2
    return jnp.where(live, slot, -1), index


def one_hot(row, count):
    return (lax.broadcasted_iota(jnp.int32, (count, row.shape[1]), 0) == row).astype(BF)


def mix_kernel(
    target_ref, hidden_hbm, gain_ref, router_ref, wq_ref, wk_ref, wv_ref,
    rows_out, gate_out, att_out,
    hidden_ref, wbuf, stats, nsend, aux, xbuf, auxbuf, pick, dense, zsend, zrecv,
    qbuf, kbuf, vbuf, att, msg, arecv, cosine, sine,
    h_sem, w_sem, w_send, w_recv,
    st_send, st_recv, x_send, x_recv, a_send, a_recv, fx_send, fa_send, gx_send, ga_send,
    z_send, z_recv, kv_send, kv_recv, m_send, m_recv,
):
    s = lax.axis_index("seq")
    m = lax.axis_index("mp")
    z, y = s // 2, s % 2
    x, c = m // 2, m % 2
    me = s * 4 + m
    weights = (wk_ref, wv_ref, wq_ref)

    def at(seq, mp):
        return {"seq": seq, "mp": mp}

    def remote(src, dst, send, recv, seq, mp):
        return pltpu.make_async_remote_copy(
            src_ref=src, dst_ref=dst, send_sem=send, recv_sem=recv,
            device_id=at(seq, mp), device_id_type=MESH,
        )

    barrier = pltpu.get_barrier_semaphore()

    @pl.loop(1, 32)
    def _(step):
        other = lax.rem(me + step, 32)
        pl.semaphore_signal(barrier, inc=1, device_id=at(other // 4, other % 4), device_id_type=MESH)

    near = s + 1 - 2 * y
    other_y = 1 - y
    hidden_copy = pltpu.make_async_copy(hidden_hbm, hidden_ref, h_sem)
    hidden_copy.start()

    def wcopy(kind):
        return remote(weights[kind], wbuf.at[kind, y], w_send.at[kind], w_recv.at[kind], near, m)

    def wlocal(kind):
        return pltpu.make_async_copy(weights[kind], wbuf.at[kind, y], w_sem.at[kind])

    pl.semaphore_wait(barrier, 31)
    wcopy(0).start()
    for kind in range(3):
        wlocal(kind).start()
    hidden_copy.wait()

    slot, index = slots_of(target_ref[...], 128)
    chosen = one_hot(slot, 256)
    rows = jnp.dot(chosen, hidden_ref[...], preferred_element_type=F32)
    rows_out[...] = rows.astype(BF)
    squares = jnp.sum(rows * rows, axis=1, keepdims=True)
    logit = jnp.sum(rows * router_ref[pl.ds(m, 1), :], axis=1, keepdims=True)
    lane = lax.broadcasted_iota(jnp.int32, (256, 128), 1)
    table = jnp.where(lane == 0, squares, jnp.where(lane == 1, logit, 0.0))
    stats[m] = table.T[0:8]
    sub = lax.broadcasted_iota(jnp.int32, (8, 1024), 0)
    place = lax.broadcasted_iota(jnp.int32, (8, 1024), 1)
    parts = jnp.where(sub == 0, index // 16, jnp.where(sub == 1, index % 16, jnp.where(
        sub == 2, place // 32, jnp.where(sub == 3, place % 32, 1))))
    parts = lax.dot_general(
        parts.astype(F32).astype(BF), chosen, (((1,), (1,)), ((), ())), preferred_element_type=F32)
    mine = jnp.where(parts[4:5] > 0.5, parts[0:1] * 16.0 + parts[1:2], -1.0)
    spot = parts[2:3] * 32.0 + parts[3:4] + (s * 1024).astype(F32)
    aux[...] = jnp.where(lax.broadcasted_iota(jnp.int32, (8, 256), 0) == 0, mine, spot)

    for step in range(1, 4):
        other = lax.rem(m + step, 4)
        remote(stats.at[m], stats.at[m], st_send.at[step - 1], st_recv.at[m], s, other).start()
    for step in range(1, 4):
        other = lax.rem(m + step, 4)
        copy = remote(stats.at[other], stats.at[other], st_send.at[step - 1], st_recv.at[other], s, other)
        copy.wait_recv()
    total = stats[0] + stats[1] + stats[2] + stats[3]
    total = jnp.concatenate([total] * 16, axis=0).T
    gate_out[...] = jnp.broadcast_to(1.0 / (1.0 + jnp.exp(-total[:, 1:2])), (256, 128))
    inverse = lax.rsqrt(total[:, 0:1] * (1.0 / 4096) + 1e-05)
    nsend[...] = (rows * inverse * gain_ref[pl.ds(m, 1), :]).astype(BF)

    here = pl.ds(pl.multiple_of(s * 128, 128), 128)

    def xcopies(half):
        seq, mp = 2 * m + half, c + 2 * lax.rem(y + half, 2)
        own = jnp.logical_and(seq == s, mp == m)
        return own, (
            remote(nsend.at[pl.ds(half * 128, 128), :], xbuf.at[here, :], x_send.at[half], x_recv.at[s], seq, mp),
            remote(aux, auxbuf.at[s], a_send.at[half], a_recv.at[s], seq, mp),
        )

    for half in range(2):
        own, pair = xcopies(half)

        @pl.when(own)
        def _():
            xbuf[here, :] = nsend[half * 128:half * 128 + 128, :]
            auxbuf[s] = aux[...]

        @pl.when(jnp.logical_not(own))
        def _():
            for copy in pair:
                copy.start()

    direct = c == z % 2

    def forward(step, to_core):
        landing = lax.rem(x + y + step // 4, 2)
        block = 2 * lax.rem(z + step, 4) + landing
        there = pl.ds(pl.multiple_of(block * 128, 128), 128)
        mp = m + 1 - 2 * c if to_core else lax.rem(m + 2, 4)
        x_sems, a_sems = (fx_send, fa_send) if to_core else (gx_send, ga_send)
        return block, (
            remote(xbuf.at[there, :], xbuf.at[there, :], x_sems.at[block], x_recv.at[block], s, mp),
            remote(auxbuf.at[block], auxbuf.at[block], a_sems.at[block], a_recv.at[block], s, mp),
        )

    @pl.loop(0, 8)
    def _(step):
        block, pair = forward(step, True)
        _, across = forward(step, False)

        @pl.when(jnp.logical_not(jnp.logical_and(jnp.logical_and(m == z, x == 0), block == s)))
        def _():
            for copy in pair:
                copy.wait_recv()

        @pl.when(jnp.logical_and(direct, step < 4))
        def _():
            for copy in across:
                copy.start()

        @pl.when(direct)
        def _():
            for copy in pair:
                copy.start()

    for kind in (1, 2):
        wcopy(kind).start()

    def line_of(which):
        return jnp.concatenate([jnp.where(
            y == 0, auxbuf[b][which:which + 1, 0:128], auxbuf[b][which:which + 1, 128:256]) for b in range(8)], axis=1)

    line = line_of(0).astype(jnp.int32)

    @pl.loop(0, 4)
    def _(tile):
        part = pl.ds(pl.multiple_of(tile * 128, 128), 128)
        hot = (lax.broadcasted_iota(jnp.int32, (128, 1024), 0) + tile * 128 == line).astype(BF)
        pick[part, :] = hot
        dense[part, :] = jnp.dot(hot, xbuf[...], preferred_element_type=F32).astype(BF)

    def zcopy(kind, step):
        peer = lax.rem(z + step, 4)
        return remote(zsend.at[kind, peer], zrecv.at[kind, z], z_send.at[kind, peer], z_recv.at[kind, z], 2 * peer + y, m)

    def zwait(kind, step):
        peer = lax.rem(z + step, 4)
        remote(zsend.at[kind, peer], zrecv.at[kind, peer], z_send.at[kind, peer], z_recv.at[kind, peer], 2 * peer + y, m).wait_recv()

    for kind in range(3):
        wlocal(kind).wait()
        remote(weights[kind], wbuf.at[kind, other_y], w_send.at[kind], w_recv.at[kind], near, m).wait_recv()

        @pl.loop(0, 2)
        def _(tile):
            part = pl.ds(pl.multiple_of(tile * 256, 256), 256)
            value = jnp.dot(
                dense[part, :], wbuf[kind].reshape(1024, 512), preferred_element_type=F32).astype(BF)
            for head in range(4):
                zsend[kind, head, part, :] = value[:, head * 128:head * 128 + 128]

        for step in range(1, 4):
            zcopy(kind, step).start()

    places = line_of(1)
    lanes = lax.broadcasted_iota(jnp.int32, (1, 128), 1) % 64
    freq = jnp.exp(-math.log(10000.0) * (2.0 * lanes.astype(F32) / 128))
    sign = jnp.where(lax.broadcasted_iota(jnp.int32, (1, 128), 1) < 64, -1.0, 1.0)

    @pl.loop(0, 4)
    def _(tile):
        part = pl.ds(pl.multiple_of(tile * 128, 128), 128)
        where = jnp.sum(pick[part, :].astype(F32) * places, axis=1, keepdims=True)
        angle = where * freq
        cosine[part, :] = jnp.cos(angle)
        sine[part, :] = jnp.sin(angle) * sign

    def kvcopy(buf, kind):
        return remote(buf.at[y], buf.at[y], kv_send.at[kind], kv_recv.at[kind], near, m)

    for kind in range(3):
        for step in range(1, 4):
            zwait(kind, step)
        value = zsend[kind, z].astype(F32)
        for step in range(1, 4):
            value = value + zrecv[kind, lax.rem(z + step, 4)].astype(F32)
        if kind != 1:
            value = value * cosine[...] + pltpu.roll(value, 64, 1) * sine[...]
        if kind == 2:
            qbuf[...] = value.astype(BF)
        else:
            buf = (kbuf, vbuf)[kind]
            buf[y] = value.astype(BF)
            kvcopy(buf, kind).start()
    for kind, buf in enumerate((kbuf, vbuf)):
        remote(buf.at[other_y], buf.at[other_y], kv_send.at[kind], kv_recv.at[kind], near, m).wait_recv()

    @pl.loop(0, 4)
    def _(tile):
        part = pl.ds(pl.multiple_of(tile * 128, 128), 128)
        keys = kbuf[...].reshape(1024, 128)
        scores = lax.dot_general(
            qbuf[part, :], keys, (((1,), (1,)), ((), ())), preferred_element_type=F32) * (1.0 / math.sqrt(HEAD_DIM))
        column = lax.broadcasted_iota(jnp.int32, (128, 1024), 1)
        rank_k = 2 * (column % 512) + column // 512
        rank_q = 2 * (lax.broadcasted_iota(jnp.int32, (128, 1024), 0) + tile * 128) + y
        allowed = rank_k <= rank_q
        scores = jnp.where(allowed, scores, -1e30)
        top = jnp.max(scores, axis=1, keepdims=True)
        weight = jnp.where(allowed, jnp.exp(scores - top), 0.0)
        total = jnp.sum(weight, axis=1, keepdims=True)
        summed = jnp.dot(weight.astype(BF), vbuf[...].reshape(1024, 128), preferred_element_type=F32)
        att[part, :] = (summed / total).astype(BF)

    messages = lax.dot_general(
        pick[...], att[...], (((0,), (0,)), ((), ())), preferred_element_type=F32)
    msg[...] = messages.astype(BF).reshape(8, 128, 128)
    part = pl.ds(pl.multiple_of(y * 128, 128), 128)
    head = m * 4 + z
    column = pl.ds(pl.multiple_of(head * 128, 128), 128)
    arecv[part, column] = msg[s]

    def mcopy(step):
        other = lax.rem(me + step, 32)
        return remote(msg.at[other // 4], arecv.at[part, column], m_send.at[other], m_recv.at[me], other // 4, other % 4)

    @pl.loop(1, 32)
    def _(step):
        mcopy(step).start()

    @pl.loop(1, 32)
    def _(step):
        other = lax.rem(me + step, 32)
        seq, mp = other // 4, other % 4
        to_part = pl.ds(pl.multiple_of(seq % 2 * 128, 128), 128)
        to_column = pl.ds(pl.multiple_of((mp * 4 + seq // 2) * 128, 128), 128)
        remote(msg.at[seq], arecv.at[to_part, to_column], m_send.at[other], m_recv.at[other], seq, mp).wait_recv()

    att_out[...] = arecv[...]

    for step in range(1, 4):
        other = lax.rem(m + step, 4)
        remote(stats.at[m], stats.at[m], st_send.at[step - 1], st_recv.at[m], s, other).wait_send()
    for half in range(2):
        own, pair = xcopies(half)

        @pl.when(jnp.logical_not(own))
        def _():
            for copy in pair:
                copy.wait_send()

    @pl.when(direct)
    def _():
        @pl.loop(0, 8)
        def _(step):
            for copy in forward(step, True)[1]:
                copy.wait_send()

            @pl.when(step < 4)
            def _():
                for copy in forward(step, False)[1]:
                    copy.wait_send()

    for kind in range(3):
        wcopy(kind).wait_send()
        for step in range(1, 4):
            zcopy(kind, step).wait_send()
    for kind, buf in enumerate((kbuf, vbuf)):
        kvcopy(buf, kind).wait_send()

    @pl.loop(1, 32)
    def _(step):
        mcopy(step).wait_send()


def finish_kernel(target_ref, hidden_ref, rows_ref, gate_ref, att_ref, w_out_ref, mixed_ref):
    slot, _ = slots_of(target_ref[...], 128)
    chosen = one_hot(slot, 256)
    flags = lax.dot_general(
        chosen, jnp.ones((256, 128), BF), (((0,), (0,)), ((), ())), preferred_element_type=F32)
    update = jnp.dot(att_ref[...], w_out_ref[...], preferred_element_type=F32)
    fresh = (rows_ref[...].astype(F32) + gate_ref[:, 0:1] * update).astype(BF)
    spread = lax.dot_general(chosen, fresh, (((0,), (0,)), ((), ())), preferred_element_type=F32)
    mixed_ref[...] = jnp.where(flags[:, 0:1] > 0.5, spread, hidden_ref[...].astype(F32)).astype(BF)


def fused(hidden, picked, target, norm_gain, router_weight, w_query, w_key, w_value, w_out):
    target = target.reshape(1, 1024)
    gain = norm_gain.reshape(4, 1024).astype(F32)
    router = router_weight.reshape(4, 1024).astype(F32)
    dma = pltpu.SemaphoreType.DMA
    rows, gate, att = pl.pallas_call(
        mix_kernel,
        out_shape=(
            jax.ShapeDtypeStruct((256, 1024), BF),
            jax.ShapeDtypeStruct((256, 128), F32),
            jax.ShapeDtypeStruct((256, 2048), BF),
        ),
        in_specs=[
            pl.BlockSpec(memory_space=pltpu.VMEM), pl.BlockSpec(memory_space=pl.ANY),
            pl.BlockSpec(memory_space=pltpu.VMEM), pl.BlockSpec(memory_space=pltpu.VMEM),
        ] + [pl.BlockSpec(memory_space=pl.ANY)] * 3,
        out_specs=[pl.BlockSpec(memory_space=pltpu.VMEM)] * 3,
        scratch_shapes=[
            pltpu.VMEM((1024, 1024), BF),
            pltpu.VMEM((3, 2, 512, 512), BF),
            pltpu.VMEM((4, 8, 256), F32),
            pltpu.VMEM((256, 1024), BF),
            pltpu.VMEM((8, 256), F32),
            pltpu.VMEM((1024, 1024), BF),
            pltpu.VMEM((8, 8, 256), F32),
            pltpu.VMEM((512, 1024), BF),
            pltpu.VMEM((512, 1024), BF),
            pltpu.VMEM((3, 4, 512, 128), BF),
            pltpu.VMEM((3, 4, 512, 128), BF),
            pltpu.VMEM((512, 128), BF),
            pltpu.VMEM((2, 512, 128), BF),
            pltpu.VMEM((2, 512, 128), BF),
            pltpu.VMEM((512, 128), BF),
            pltpu.VMEM((8, 128, 128), BF),
            pltpu.VMEM((256, 2048), BF),
            pltpu.VMEM((512, 128), F32),
            pltpu.VMEM((512, 128), F32),
            dma(()), dma((3,)), dma((3,)), dma((3,)),
            dma((3,)), dma((4,)), dma((2,)), dma((8,)), dma((2,)), dma((8,)), dma((8,)), dma((8,)), dma((8,)), dma((8,)),
            dma((3, 4)), dma((3, 4)), dma((2,)), dma((2,)), dma((32,)), dma((32,)),
        ],
        compiler_params=pltpu.CompilerParams(
            collective_id=0, has_side_effects=True, vmem_limit_bytes=48 * 2 ** 20),
    )(target, hidden, gain, router, w_query, w_key, w_value)
    return pl.pallas_call(
        finish_kernel,
        out_shape=jax.ShapeDtypeStruct((1024, 1024), BF),
        in_specs=[pl.BlockSpec(memory_space=pltpu.VMEM)] * 6,
        out_specs=pl.BlockSpec(memory_space=pltpu.VMEM),
        compiler_params=pltpu.CompilerParams(vmem_limit_bytes=48 * 2 ** 20),
    )(target, hidden, rows, gate, att, w_out)


def per_device(hidden, picked, target, *rest):
    small = (
        lax.axis_size("seq") == 8 and lax.axis_size("mp") == 4
        and hidden.shape == (1024, 1024) and picked.shape[0] == 128
    )
    return (fused if small else general)(hidden, picked, target, *rest)


def solution(mesh):
    placed = (
        P("seq", "mp"),
        P("seq"),
        P("seq"),
        P(),
        P(),
        P("seq", "mp"),
        P("seq", "mp"),
        P("seq", "mp"),
        P(None, "mp"),
    )
    return jax.shard_map(
        per_device, mesh=mesh, in_specs=placed, out_specs=P("seq", "mp"), check_vma=False
    )
```
